32 devices in a mesh: parts: 2 (over x), wide: 16 (over z, y, core).
Axes of the slice: x: 2, y: 2, z: 4, core: 2. Of those that a mesh axis runs over, the one named last changes fastest.
Arguments:
- hidden_grads: bfloat16 [512, 14784], P(('parts', 'wide')), parts along dimension 0, may hold values from -400 to 400
- tile_slot: int32 [156], P('parts'), parts along dimension 0, may hold values from 0 to 79, as said below
Outputs:
- factor_tiles: float32 [160, 1232, 1232], P(('parts', 'wide')), parts along dimension 0
The draws below stay inside these ranges and needn't reach their ends.
There are 2 independent parts, one for each index of `parts`. The reference program is written for one: setup_inputs(seed, part) draws one part's arguments, and reference() takes and returns one part's arrays. A program takes and returns all parts, laid end to end along the dimension named above; each array names one. Nothing has to cross between parts.
Inputs may be any that keep to these rules, and one draw needn't show every extreme that they name: `tile_slot`: entries are distinct. The device of slot s is s // 5; some device owns exactly 5 tiles.
All inputs are finite; a program needn't handle non-finite values.
Results may differ from the reference program's by a relative error of at most 0.0003.
Values may be sent and summed in bfloat16 or wider, within the bound.
A program may use at most 128 MiB of HBM per device.

```python
import math
import jax
import jax.numpy as jnp
import numpy as np
from jax import lax

FF = 14784
P_SIZE = 1232
TOKENS = 256
NP = 12
TILES = 78
SLOTS = 5
N_WIDE = 16


def draw_hidden_grads(key, part):
    key = jax.random.fold_in(key, 11)
    noise_key, row_key, col_key = jax.random.split(key, 3)
    position = jnp.arange(TOKENS, dtype=jnp.float32) / max(TOKENS - 1, 1)
    row_scale = jnp.exp(jax.random.uniform(row_key, (TOKENS, 1), jnp.float32, math.log(0.5), math.log(5.0)))
    col_scale = jnp.exp(jax.random.uniform(col_key, (1, FF), jnp.float32, math.log(0.5), math.log(5.0)))
    base_noise = jnp.clip(jax.random.normal(noise_key, (TOKENS, FF), jnp.float32), -4.0, 4.0)
    token_ramp = 1.0 + 2.0 * position
    values = base_noise * row_scale * col_scale * token_ramp[:, None]
    return values.astype(jnp.bfloat16)


def draw_tile_slot(key, part):
    key = jax.random.fold_in(key, 5)
    owner_key, rank_key, order_key = jax.random.split(key, 3)
    capacity = N_WIDE * SLOTS
    full_owner = jax.random.randint(owner_key, (), 0, N_WIDE)
    slot_rank = jax.random.permutation(rank_key, capacity).astype(jnp.int32)
    slot_number = jnp.arange(capacity, dtype=jnp.int32)
    scores = jnp.where(slot_number // SLOTS == full_owner, slot_number % SLOTS - SLOTS, slot_rank)
    ordered = jnp.argsort(scores, stable=True).astype(jnp.int32)
    chosen = ordered[:TILES]
    return jax.random.permutation(order_key, chosen).astype(jnp.int32)


def setup_inputs(seed: int = 0, part: int = 0) -> dict:
    splits = jax.random.split(jax.random.key(seed), 3)
    own_keys = jax.random.split(jax.random.fold_in(splits[2], part), 3)
    return {
        "hidden_grads": draw_hidden_grads(jax.random.fold_in(jax.random.fold_in(splits[2], part), 71), part),
        "tile_slot": draw_tile_slot(jax.random.fold_in(jax.random.fold_in(splits[2], part), 71), part),
    }


DAMPING = 0.1


def reference(hidden_grads, tile_slot):
    square_sum = jnp.sum(jnp.square(hidden_grads.astype(jnp.float32)))
    upper_rows, upper_cols = np.triu_indices(NP)
    row_table = jnp.asarray(upper_rows, jnp.int32)
    col_table = jnp.asarray(upper_cols, jnp.int32)
    scale_factor = FF / square_sum
    identity_tile = jnp.eye(P_SIZE, dtype=jnp.float32)

    def one_tile(index):
        row_panel = row_table[index]
        col_panel = col_table[index]
        left_cols = lax.dynamic_slice_in_dim(hidden_grads, (row_panel * P_SIZE).astype(jnp.int32), P_SIZE, 1)
        right_cols = lax.dynamic_slice_in_dim(hidden_grads, (col_panel * P_SIZE).astype(jnp.int32), P_SIZE, 1)
        gram = jnp.dot(left_cols.T, right_cols, preferred_element_type=jnp.float32)
        on_diag = (row_panel == col_panel).astype(jnp.float32)
        return gram * scale_factor + DAMPING * identity_tile * on_diag

    tiles = lax.map(one_tile, jnp.arange(TILES, dtype=jnp.int32))
    return jnp.zeros((N_WIDE * SLOTS, P_SIZE, P_SIZE), jnp.float32).at[tile_slot].set(tiles)
```

```python
import functools

import jax
import jax.numpy as jnp
import numpy as np
from jax import lax
from jax.experimental import pallas as pl
from jax.experimental.pallas import tpu as pltpu
from jax.sharding import PartitionSpec as P

FF = 14784
P_SIZE = 1232
NP = 12
TILES = 78
DAMPING = 0.1

P_PAD = 1280
CHUNKS = 4
CHUNK_PANELS = NP // CHUNKS
ROW_BLOCK = 256
MESH = pl.DeviceIdType.MESH


def ring_position(chip, chips):
    if chips != 8:
        return chip
    depth, side = chip // 2, chip % 2
    return depth + side * (chips - 1 - 2 * depth)


def ring_chip(position, chips):
    if chips != 8:
        return position
    side = position // (chips // 2)
    depth = position + side * (chips - 1 - 2 * position)
    return 2 * depth + side


def gather_kernel(n, slot_count, grads_ref, slot_ref, panels, codes_ref, scale_ref,
                  squares, ring_send, ring_recv, sib_send, sib_recv):
    chips = n // 2
    half = chips // 2
    rows = grads_ref.shape[0]
    me = lax.axis_index("wide")
    core = me % 2
    pos = ring_position(me // 2, chips)

    def device_at(position, which):
        return ring_chip(position % chips, chips) * 2 + which

    targets = (device_at(pos + 1, core), device_at(pos + chips - 1, core))
    sibling = me + 1 - 2 * core

    barrier = pltpu.get_barrier_semaphore()
    for peer in (*targets, sibling):
        pl.semaphore_signal(barrier, inc=1, device_id={"wide": peer}, device_id_type=MESH)

    mine = pl.ds(pl.multiple_of(me * rows, 16), rows)
    for p in range(NP):
        panels[p, mine, :P_SIZE] = grads_ref[:, p * P_SIZE:(p + 1) * P_SIZE]
        panels[p, mine, P_SIZE:] = jnp.zeros((rows, P_PAD - P_SIZE), jnp.bfloat16)

    def block(device, chunk):
        row = pl.multiple_of(device * rows, 16)
        return panels.at[pl.ds(chunk * CHUNK_PANELS, CHUNK_PANELS), pl.ds(row, rows), :]

    def owner(direction, hop, which):
        shift = chips - hop if direction == 0 else hop
        return device_at(pos + shift, which)

    def ring_copy(direction, hop, chunk):
        ref = block(owner(direction, hop, core), chunk)
        return pltpu.make_async_remote_copy(
            src_ref=ref, dst_ref=ref,
            send_sem=ring_send.at[direction, hop, chunk],
            recv_sem=ring_recv.at[direction, hop, chunk],
            device_id={"wide": targets[direction]}, device_id_type=MESH)

    def ring_arrival(direction, hop, chunk):
        ref = block(owner(direction, hop, core), chunk)
        return pltpu.make_async_remote_copy(
            src_ref=ref, dst_ref=ref,
            send_sem=ring_send.at[direction, hop - 1, chunk],
            recv_sem=ring_recv.at[direction, hop - 1, chunk],
            device_id={"wide": targets[direction]}, device_id_type=MESH)

    def sib_copy(direction, hop, chunk, which):
        ref = block(owner(direction, hop, which), chunk)
        return pltpu.make_async_remote_copy(
            src_ref=ref, dst_ref=ref,
            send_sem=sib_send.at[direction, hop, chunk],
            recv_sem=sib_recv.at[direction, hop, chunk],
            device_id={"wide": sibling}, device_id_type=MESH)

    def add_squares(device, chunk):
        row = pl.multiple_of(device * rows, 16)
        total = squares[...]
        for p in range(CHUNK_PANELS):
            values = panels[chunk * CHUNK_PANELS + p, pl.ds(row, rows), :].astype(jnp.float32)
            values = values * values
            for k in range(P_PAD // 128):
                total = total + values[:, k * 128:(k + 1) * 128]
        squares[...] = total

    def halves(direction):
        return range(CHUNKS // 2) if direction == 0 else range(CHUNKS // 2, CHUNKS)

    pl.semaphore_wait(barrier, 3)
    for chunk in range(CHUNKS):
        for direction in range(2):
            ring_copy(direction, 0, chunk).start()
    for chunk in range(CHUNKS):
        sib_copy(0, 0, chunk, core).start()

    squares[...] = jnp.zeros_like(squares)
    for chunk in range(CHUNKS):
        add_squares(me, chunk)
    lane = lax.broadcasted_iota(jnp.int32, (8, 128), 1) + me * slot_count
    codes = jnp.zeros((8, 128), jnp.int32)
    for t, (i, j) in enumerate(zip(*np.triu_indices(NP))):
        codes = jnp.where(lane == slot_ref[t], int(1 + i * NP + j), codes)
    codes_ref[...] = codes
    for chunk in range(CHUNKS):
        sib_copy(0, 0, chunk, 1 - core).wait_recv()
        add_squares(sibling, chunk)

    def drain_sibling(hop, chunk, direction):
        sib_copy(direction, hop, chunk, 1 - core).wait_recv()
        add_squares(owner(direction, hop, 1 - core), chunk)

    for hop in range(1, half + 1):
        for chunk in range(CHUNKS):
            for direction in range(2):
                if hop < half or chunk in halves(direction):
                    ring_arrival(direction, hop, chunk).wait_recv()
                    if hop + 1 < half or (hop + 1 == half and chunk in halves(direction)):
                        ring_copy(direction, hop, chunk).start()
                    sib_copy(direction, hop, chunk, core).start()
            for direction in range(2):
                if hop < half or chunk in halves(direction):
                    add_squares(owner(direction, hop, core), chunk)
                    if hop > 1:
                        drain_sibling(hop - 1, chunk, direction)
                elif hop > 1:
                    drain_sibling(hop - 1, chunk, direction)
    for direction in range(2):
        for chunk in halves(direction):
            drain_sibling(half, chunk, direction)

    scale_ref[...] = jnp.full((8, 128), FF / jnp.sum(squares[...]), jnp.float32)

    for chunk in range(CHUNKS):
        sib_copy(0, 0, chunk, core).wait_send()
    for hop in range(half + 1):
        for direction in range(2):
            for chunk in range(CHUNKS):
                if hop + 1 < half or (hop + 1 == half and chunk in halves(direction)):
                    ring_copy(direction, hop, chunk).wait_send()
                if 1 <= hop < half or (hop == half and chunk in halves(direction)):
                    sib_copy(direction, hop, chunk, core).wait_send()


def gather(grads, tile_slot, n, slot_count):
    rows = grads.shape[0]
    hops = n // 4 + 1
    vmem = pl.BlockSpec(memory_space=pltpu.VMEM)
    return pl.pallas_call(
        functools.partial(gather_kernel, n, slot_count),
        out_shape=[
            pltpu.VMEM((NP, n * rows, P_PAD), jnp.bfloat16),
            jax.ShapeDtypeStruct((8, 128), jnp.int32),
            jax.ShapeDtypeStruct((8, 128), jnp.float32),
        ],
        in_specs=[vmem, pl.BlockSpec(memory_space=pltpu.SMEM)],
        out_specs=[vmem, vmem, vmem],
        scratch_shapes=[
            pltpu.VMEM((rows, 128), jnp.float32),
            pltpu.SemaphoreType.DMA((2, hops, CHUNKS)),
            pltpu.SemaphoreType.DMA((2, hops, CHUNKS)),
            pltpu.SemaphoreType.DMA((2, hops, CHUNKS)),
            pltpu.SemaphoreType.DMA((2, hops, CHUNKS)),
        ],
        compiler_params=pltpu.CompilerParams(
            collective_id=0, has_side_effects=True, vmem_limit_bytes=20 * 2**20),
        name="gather_panels",
    )(grads, tile_slot)


def tile_kernel(codes_ref, panels, scale_ref, out_ref):
    code = codes_ref[0, pl.program_id(0)]
    step = pl.program_id(1)

    @pl.when(code == 0)
    def _():
        out_ref[...] = jnp.zeros_like(out_ref)

    @pl.when(code > 0)
    def _():
        left, right = (code - 1) // NP, (code - 1) % NP
        first = pl.multiple_of(step * ROW_BLOCK, ROW_BLOCK)
        gram = lax.dot_general(
            panels[left, :, pl.ds(first, ROW_BLOCK)], panels[right],
            (((0,), (0,)), ((), ())), preferred_element_type=jnp.float32)
        out_ref[0] = gram[:, :P_SIZE] * scale_ref[0, 0]

        @pl.when(left == right)
        def _():
            here = pl.ds(first, ROW_BLOCK)
            row = lax.broadcasted_iota(jnp.int32, (ROW_BLOCK, P_SIZE), 0) + first
            col = lax.broadcasted_iota(jnp.int32, (ROW_BLOCK, P_SIZE), 1)
            out_ref[0] = out_ref[0] + jnp.where(row == col, DAMPING, 0.0)


def make_tiles(codes, panels, scale, slot_count):
    vmem = pl.BlockSpec(memory_space=pltpu.VMEM)
    return pl.pallas_call(
        tile_kernel,
        out_shape=jax.ShapeDtypeStruct((slot_count, P_SIZE, P_SIZE), jnp.float32),
        grid_spec=pltpu.PrefetchScalarGridSpec(
            num_scalar_prefetch=1,
            grid=(slot_count, pl.cdiv(P_SIZE, ROW_BLOCK)),
            in_specs=[vmem, vmem],
            out_specs=pl.BlockSpec((1, ROW_BLOCK, P_SIZE), lambda s, r, codes: (s, r, 0)),
        ),
        compiler_params=pltpu.CompilerParams(vmem_limit_bytes=20 * 2**20),
        name="factor_tiles",
    )(codes, panels, scale)


def shards(grads, tile_slot):
    n = lax.axis_size("wide")
    slot_count = (TILES + n - 1) // n
    panels, codes, scale = gather(grads, tile_slot, n, slot_count)
    return make_tiles(codes, panels, scale, slot_count)


def solution(mesh):
    in_specs = (P(("parts", "wide"), None), P("parts"))
    out_specs = P(("parts", "wide"), None, None)
    return jax.shard_map(shards, mesh=mesh, in_specs=in_specs, out_specs=out_specs, check_vma=False)
```

```python
import functools

import jax
import jax.numpy as jnp
import numpy as np
from jax import lax
from jax.experimental import pallas as pl
from jax.experimental.pallas import tpu as pltpu
from jax.sharding import PartitionSpec as P

FF = 14784
P_SIZE = 1232
NP = 12
TILES = 78
DAMPING = 0.1

P_PAD = 1280
CHUNKS = 4
CHUNK_PANELS = NP // CHUNKS
ROW_BLOCK = 256
TILE_BUFFERS = 6
VMEM_BYTES = 64 * 2**20
MESH = pl.DeviceIdType.MESH


def ring_position(chip, chips):
    if chips != 8:
        return chip
    depth, side = chip // 2, chip % 2
    return depth + side * (chips - 1 - 2 * depth)


def ring_chip(position, chips):
    if chips != 8:
        return position
    side = position // (chips // 2)
    depth = position + side * (chips - 1 - 2 * position)
    return 2 * depth + side


def gather_kernel(n, slot_count, grads_hbm, slot_hbm, panels, codes_ref, scale_ref,
                  grads_ref, slot_ref, squares, arg_sems, ring_send, ring_recv, sib_send, sib_recv):
    chips = n // 2
    half = chips // 2
    rows = grads_ref.shape[0]
    fetch_grads = pltpu.make_async_copy(grads_hbm, grads_ref, arg_sems.at[0])
    fetch_slots = pltpu.make_async_copy(slot_hbm, slot_ref, arg_sems.at[1])
    fetch_grads.start()
    fetch_slots.start()
    me = lax.axis_index("wide")
    core = me % 2
    pos = ring_position(me // 2, chips)

    def device_at(position, which):
        return ring_chip(position % chips, chips) * 2 + which

    targets = (device_at(pos + 1, core), device_at(pos + chips - 1, core))
    sibling = me + 1 - 2 * core

    barrier = pltpu.get_barrier_semaphore()
    for peer in (*targets, sibling):
        pl.semaphore_signal(barrier, inc=1, device_id={"wide": peer}, device_id_type=MESH)

    mine = pl.ds(pl.multiple_of(me * rows, 16), rows)

    def block(device, chunk):
        row = pl.multiple_of(device * rows, 16)
        return panels.at[pl.ds(chunk * CHUNK_PANELS, CHUNK_PANELS), pl.ds(row, rows), :]

    def owner(direction, hop, which):
        shift = chips - hop if direction == 0 else hop
        return device_at(pos + shift, which)

    def ring_copy(direction, hop, chunk):
        ref = block(owner(direction, hop, core), chunk)
        return pltpu.make_async_remote_copy(
            src_ref=ref, dst_ref=ref,
            send_sem=ring_send.at[direction, hop, chunk],
            recv_sem=ring_recv.at[direction, hop, chunk],
            device_id={"wide": targets[direction]}, device_id_type=MESH)

    def ring_arrival(direction, hop, chunk):
        ref = block(owner(direction, hop, core), chunk)
        return pltpu.make_async_remote_copy(
            src_ref=ref, dst_ref=ref,
            send_sem=ring_send.at[direction, hop - 1, chunk],
            recv_sem=ring_recv.at[direction, hop - 1, chunk],
            device_id={"wide": targets[direction]}, device_id_type=MESH)

    def sib_copy(direction, hop, chunk, which):
        ref = block(owner(direction, hop, which), chunk)
        return pltpu.make_async_remote_copy(
            src_ref=ref, dst_ref=ref,
            send_sem=sib_send.at[direction, hop, chunk],
            recv_sem=sib_recv.at[direction, hop, chunk],
            device_id={"wide": sibling}, device_id_type=MESH)

    def add_squares(device, chunk):
        row = pl.multiple_of(device * rows, 16)
        total = squares[...]
        for p in range(CHUNK_PANELS):
            values = panels[chunk * CHUNK_PANELS + p, pl.ds(row, rows), :].astype(jnp.float32)
            values = values * values
            for k in range(P_PAD // 128):
                total = total + values[:, k * 128:(k + 1) * 128]
        squares[...] = total

    def halves(direction):
        return range(CHUNKS // 2) if direction == 0 else range(CHUNKS // 2, CHUNKS)

    fetch_grads.wait()
    for chunk in range(CHUNKS):
        for p in range(chunk * CHUNK_PANELS, (chunk + 1) * CHUNK_PANELS):
            panels[p, mine, :P_SIZE] = grads_ref[:, p * P_SIZE:(p + 1) * P_SIZE]
            panels[p, mine, P_SIZE:] = jnp.zeros((rows, P_PAD - P_SIZE), jnp.bfloat16)
        if chunk == 0:
            pl.semaphore_wait(barrier, 3)
        for direction in range(2):
            ring_copy(direction, 0, chunk).start()
    for chunk in range(CHUNKS):
        sib_copy(0, 0, chunk, core).start()

    squares[...] = jnp.zeros_like(squares)
    for chunk in range(CHUNKS):
        add_squares(me, chunk)
    fetch_slots.wait()
    lane = lax.broadcasted_iota(jnp.int32, (8, 128), 1) + me * slot_count
    codes = jnp.zeros((8, 128), jnp.int32)
    for t, (i, j) in enumerate(zip(*np.triu_indices(NP))):
        codes = jnp.where(lane == slot_ref[t], int(1 + i * NP + j), codes)
    codes_ref[...] = codes
    for chunk in range(CHUNKS):
        sib_copy(0, 0, chunk, 1 - core).wait_recv()
        add_squares(sibling, chunk)

    def drain_sibling(hop, chunk, direction):
        sib_copy(direction, hop, chunk, 1 - core).wait_recv()
        add_squares(owner(direction, hop, 1 - core), chunk)

    for hop in range(1, half + 1):
        for chunk in range(CHUNKS):
            for direction in range(2):
                if hop < half or chunk in halves(direction):
                    ring_arrival(direction, hop, chunk).wait_recv()
                    if hop + 1 < half or (hop + 1 == half and chunk in halves(direction)):
                        ring_copy(direction, hop, chunk).start()
                    sib_copy(direction, hop, chunk, core).start()
            for direction in range(2):
                if hop < half or chunk in halves(direction):
                    add_squares(owner(direction, hop, core), chunk)
                    if hop > 1:
                        drain_sibling(hop - 1, chunk, direction)
                elif hop > 1:
                    drain_sibling(hop - 1, chunk, direction)
    for direction in range(2):
        for chunk in halves(direction):
            drain_sibling(half, chunk, direction)

    scale_ref[...] = jnp.full((8, 128), FF / jnp.sum(squares[...]), jnp.float32)

    for chunk in range(CHUNKS):
        sib_copy(0, 0, chunk, core).wait_send()
    for hop in range(half + 1):
        for direction in range(2):
            for chunk in range(CHUNKS):
                if hop + 1 < half or (hop + 1 == half and chunk in halves(direction)):
                    ring_copy(direction, hop, chunk).wait_send()
                if 1 <= hop < half or (hop == half and chunk in halves(direction)):
                    sib_copy(direction, hop, chunk, core).wait_send()


def gather(grads, tile_slot, n, slot_count):
    rows = grads.shape[0]
    hops = n // 4 + 1
    vmem = pl.BlockSpec(memory_space=pltpu.VMEM)
    return pl.pallas_call(
        functools.partial(gather_kernel, n, slot_count),
        out_shape=[
            pltpu.VMEM((NP, n * rows, P_PAD), jnp.bfloat16),
            pltpu.VMEM((8, 128), jnp.int32),
            pltpu.VMEM((8, 128), jnp.float32),
        ],
        in_specs=[pl.BlockSpec(memory_space=pltpu.HBM)] * 2,
        out_specs=[vmem, vmem, vmem],
        scratch_shapes=[
            pltpu.VMEM(grads.shape, jnp.bfloat16),
            pltpu.SMEM(tile_slot.shape, jnp.int32),
            pltpu.VMEM((rows, 128), jnp.float32),
            pltpu.SemaphoreType.DMA((2,)),
            pltpu.SemaphoreType.DMA((2, hops, CHUNKS)),
            pltpu.SemaphoreType.DMA((2, hops, CHUNKS)),
            pltpu.SemaphoreType.DMA((2, hops, CHUNKS)),
            pltpu.SemaphoreType.DMA((2, hops, CHUNKS)),
        ],
        compiler_params=pltpu.CompilerParams(
            collective_id=0, has_side_effects=True,
            vmem_limit_bytes=VMEM_BYTES - 2 * NP * n * rows * P_PAD - 2**18),
        name="gather_panels",
    )(grads, tile_slot)


def tile_kernel(slot_count, codes_ref, panels, scale_ref, out, tiles, sems):
    starts = list(range(0, P_SIZE, ROW_BLOCK))

    def write(step):
        slot, first = step // len(starts), starts[step % len(starts)]
        rows = min(ROW_BLOCK, P_SIZE - first)
        return pltpu.make_async_copy(
            tiles.at[step % TILE_BUFFERS, :rows, :], out.at[slot, pl.ds(first, rows), :],
            sems.at[step % TILE_BUFFERS])

    for slot in range(slot_count):
        code = codes_ref[0, slot]
        tile = jnp.maximum(code - 1, 0)
        left, right = tile // NP, tile % NP
        scale = jnp.where(code > 0, scale_ref[0, 0], 0.0)
        damping = jnp.where(jnp.logical_and(left == right, code > 0), DAMPING, 0.0)
        for block, first in enumerate(starts):
            rows = min(ROW_BLOCK, P_SIZE - first)
            step = slot * len(starts) + block
            buffer = step % TILE_BUFFERS
            if step >= TILE_BUFFERS:
                write(step - TILE_BUFFERS).wait()
            gram = lax.dot_general(
                panels[left, :, first:first + ROW_BLOCK], panels[right],
                (((0,), (0,)), ((), ())), preferred_element_type=jnp.float32)
            factor = gram[:rows, :P_SIZE] * scale
            tiles[buffer, :rows, :] = factor
            last = min(first + ROW_BLOCK, P_SIZE)
            row = lax.broadcasted_iota(jnp.int32, (rows, last - first), 0)
            col = lax.broadcasted_iota(jnp.int32, (rows, last - first), 1)
            tiles[buffer, :rows, first:last] = (
                factor[:, first:last] + jnp.where(row == col, damping, 0.0))
            write(step).start()
    steps = slot_count * len(starts)
    for step in range(max(0, steps - TILE_BUFFERS), steps):
        write(step).wait()


def make_tiles(codes, panels, scale, slot_count):
    vmem = pl.BlockSpec(memory_space=pltpu.VMEM)
    return pl.pallas_call(
        functools.partial(tile_kernel, slot_count),
        out_shape=jax.ShapeDtypeStruct((slot_count, P_SIZE, P_SIZE), jnp.float32),
        in_specs=[pl.BlockSpec(memory_space=pltpu.SMEM), vmem, vmem],
        out_specs=pl.BlockSpec(memory_space=pl.ANY),
        scratch_shapes=[
            pltpu.VMEM((TILE_BUFFERS, ROW_BLOCK, P_SIZE), jnp.float32),
            pltpu.SemaphoreType.DMA((TILE_BUFFERS,)),
        ],
        compiler_params=pltpu.CompilerParams(vmem_limit_bytes=20 * 2**20),
        name="factor_tiles",
    )(codes, panels, scale)


def shards(grads, tile_slot):
    n = lax.axis_size("wide")
    slot_count = (TILES + n - 1) // n
    panels, codes, scale = gather(grads, tile_slot, n, slot_count)
    return make_tiles(codes, panels, scale, slot_count)


def solution(mesh):
    in_specs = (P(("parts", "wide"), None), P("parts"))
    out_specs = P(("parts", "wide"), None, None)
    return jax.shard_map(shards, mesh=mesh, in_specs=in_specs, out_specs=out_specs, check_vma=False)
```

```python
import functools

import jax
import jax.numpy as jnp
import numpy as np
from jax import lax
from jax.experimental import pallas as pl
from jax.experimental.pallas import tpu as pltpu
from jax.sharding import PartitionSpec as P

FF = 14784
P_SIZE = 1232
NP = 12
TILES = 78
DAMPING = 0.1

P_PAD = 1280
CHUNKS = 4
CHUNK_COLS = 3712
ROW_BLOCK = 256
TILE_BUFFERS = 6
VMEM_BYTES = 64 * 2**20
MESH = pl.DeviceIdType.MESH


def ring_position(chip, chips):
    if chips != 8:
        return chip
    depth, side = chip // 2, chip % 2
    return depth + side * (chips - 1 - 2 * depth)


def ring_chip(position, chips):
    if chips != 8:
        return position
    side = position // (chips // 2)
    depth = position + side * (chips - 1 - 2 * position)
    return 2 * depth + side


def gather_kernel(n, slot_count, grads_hbm, slot_hbm, panels, codes_ref, scale_ref,
                  raw, slot_ref, squares, arg_sems, ring_send, ring_recv, sib_send, sib_recv):
    chips = n // 2
    half = chips // 2
    rows = grads_hbm.shape[0]
    me = lax.axis_index("wide")
    mine = pl.ds(pl.multiple_of(me * rows, 16), rows)
    fetch_grads = pltpu.make_async_copy(grads_hbm, raw.at[mine, :], arg_sems.at[0])
    fetch_slots = pltpu.make_async_copy(slot_hbm, slot_ref, arg_sems.at[1])
    fetch_grads.start()
    fetch_slots.start()
    core = me % 2
    pos = ring_position(me // 2, chips)

    def device_at(position, which):
        return ring_chip(position % chips, chips) * 2 + which

    targets = (device_at(pos + 1, core), device_at(pos + chips - 1, core))
    sibling = me + 1 - 2 * core

    barrier = pltpu.get_barrier_semaphore()
    for peer in (*targets, sibling):
        pl.semaphore_signal(barrier, inc=1, device_id={"wide": peer}, device_id_type=MESH)

    def columns(chunk):
        return chunk * CHUNK_COLS, min((chunk + 1) * CHUNK_COLS, FF)

    def block(device, chunk):
        first, last = columns(chunk)
        row = pl.multiple_of(device * rows, 16)
        return raw.at[pl.ds(row, rows), first:last]

    def source(device, hop, chunk):
        first, last = columns(chunk)
        return block(device, chunk) if hop else grads_hbm.at[:, first:last]

    def owner(direction, hop, which):
        shift = chips - hop if direction == 0 else hop
        return device_at(pos + shift, which)

    def ring_copy(direction, hop, chunk):
        device = owner(direction, hop, core)
        return pltpu.make_async_remote_copy(
            src_ref=source(device, hop, chunk), dst_ref=block(device, chunk),
            send_sem=ring_send.at[direction, hop, chunk],
            recv_sem=ring_recv.at[direction, hop, chunk],
            device_id={"wide": targets[direction]}, device_id_type=MESH)

    def ring_arrival(direction, hop, chunk):
        ref = block(owner(direction, hop, core), chunk)
        return pltpu.make_async_remote_copy(
            src_ref=ref, dst_ref=ref,
            send_sem=ring_send.at[direction, hop - 1, chunk],
            recv_sem=ring_recv.at[direction, hop - 1, chunk],
            device_id={"wide": targets[direction]}, device_id_type=MESH)

    def sib_copy(direction, hop, chunk, which):
        device = owner(direction, hop, which)
        return pltpu.make_async_remote_copy(
            src_ref=source(device, hop, chunk), dst_ref=block(device, chunk),
            send_sem=sib_send.at[direction, hop, chunk],
            recv_sem=sib_recv.at[direction, hop, chunk],
            device_id={"wide": sibling}, device_id_type=MESH)

    def take(device, chunk):
        first, last = columns(chunk)
        here = pl.ds(pl.multiple_of(device * rows, 16), rows)
        for p in range(NP):
            start, stop = max(p * P_SIZE, first), min((p + 1) * P_SIZE, last)
            if start < stop:
                panels[p, here, start - p * P_SIZE:stop - p * P_SIZE] = raw[here, start:stop]
        whole = (last - first) // 128 * 128
        values = raw[here, first:first + whole].astype(jnp.float32)
        values = values * values
        total = squares[...]
        for k in range(0, whole, 128):
            total = total + values[:, k:k + 128]
        squares[...] = total
        rest = last - first - whole
        if rest:
            values = raw[here, first + whole:last].astype(jnp.float32)
            squares[:, :rest] = squares[:, :rest] + values * values

    def halves(direction):
        return range(CHUNKS // 2) if direction == 0 else range(CHUNKS // 2, CHUNKS)

    pl.semaphore_wait(barrier, 3)
    for chunk in range(CHUNKS):
        for direction in range(2):
            ring_copy(direction, 0, chunk).start()
    for chunk in range(CHUNKS):
        sib_copy(0, 0, chunk, core).start()

    squares[...] = jnp.zeros_like(squares)
    fetch_grads.wait()
    for chunk in range(CHUNKS):
        take(me, chunk)
    fetch_slots.wait()
    lane = lax.broadcasted_iota(jnp.int32, (8, 128), 1) + me * slot_count
    codes = jnp.zeros((8, 128), jnp.int32)
    for t, (i, j) in enumerate(zip(*np.triu_indices(NP))):
        codes = jnp.where(lane == slot_ref[t], int(1 + i * NP + j), codes)
    codes_ref[...] = codes
    for chunk in range(CHUNKS):
        sib_copy(0, 0, chunk, 1 - core).wait_recv()
        take(sibling, chunk)

    def drain_sibling(hop, chunk, direction):
        sib_copy(direction, hop, chunk, 1 - core).wait_recv()
        take(owner(direction, hop, 1 - core), chunk)

    for hop in range(1, half + 1):
        for chunk in range(CHUNKS):
            for direction in range(2):
                if hop < half or chunk in halves(direction):
                    ring_arrival(direction, hop, chunk).wait_recv()
                    if hop + 1 < half or (hop + 1 == half and chunk in halves(direction)):
                        ring_copy(direction, hop, chunk).start()
                    sib_copy(direction, hop, chunk, core).start()
            for direction in range(2):
                if hop < half or chunk in halves(direction):
                    take(owner(direction, hop, core), chunk)
                    if hop > 1:
                        drain_sibling(hop - 1, chunk, direction)
                elif hop > 1:
                    drain_sibling(hop - 1, chunk, direction)
    for direction in range(2):
        for chunk in halves(direction):
            drain_sibling(half, chunk, direction)

    scale_ref[...] = jnp.full((8, 128), FF / jnp.sum(squares[...]), jnp.float32)

    for chunk in range(CHUNKS):
        sib_copy(0, 0, chunk, core).wait_send()
    for hop in range(half + 1):
        for direction in range(2):
            for chunk in range(CHUNKS):
                if hop + 1 < half or (hop + 1 == half and chunk in halves(direction)):
                    ring_copy(direction, hop, chunk).wait_send()
                if 1 <= hop < half or (hop == half and chunk in halves(direction)):
                    sib_copy(direction, hop, chunk, core).wait_send()


def gather(grads, tile_slot, n, slot_count):
    rows = grads.shape[0]
    hops = n // 4 + 1
    vmem = pl.BlockSpec(memory_space=pltpu.VMEM)
    return pl.pallas_call(
        functools.partial(gather_kernel, n, slot_count),
        out_shape=[
            pltpu.VMEM((NP, n * rows, P_PAD), jnp.bfloat16),
            pltpu.VMEM((8, 128), jnp.int32),
            pltpu.VMEM((8, 128), jnp.float32),
        ],
        in_specs=[pl.BlockSpec(memory_space=pltpu.HBM)] * 2,
        out_specs=[vmem, vmem, vmem],
        scratch_shapes=[
            pltpu.VMEM((n * rows, FF), jnp.bfloat16),
            pltpu.SMEM(tile_slot.shape, jnp.int32),
            pltpu.VMEM((rows, 128), jnp.float32),
            pltpu.SemaphoreType.DMA((2,)),
            pltpu.SemaphoreType.DMA((2, hops, CHUNKS)),
            pltpu.SemaphoreType.DMA((2, hops, CHUNKS)),
            pltpu.SemaphoreType.DMA((2, hops, CHUNKS)),
            pltpu.SemaphoreType.DMA((2, hops, CHUNKS)),
        ],
        compiler_params=pltpu.CompilerParams(
            collective_id=0, has_side_effects=True,
            vmem_limit_bytes=VMEM_BYTES - 2 * NP * n * rows * P_PAD - 2**18),
        name="gather_panels",
    )(grads, tile_slot)


def tile_kernel(slot_count, codes_ref, panels, scale_ref, out, tiles, sems):
    starts = list(range(0, P_SIZE, ROW_BLOCK))

    def write(step):
        slot, first = step // len(starts), starts[step % len(starts)]
        rows = min(ROW_BLOCK, P_SIZE - first)
        return pltpu.make_async_copy(
            tiles.at[step % TILE_BUFFERS, :rows, :], out.at[slot, pl.ds(first, rows), :],
            sems.at[step % TILE_BUFFERS])

    for slot in range(slot_count):
        code = codes_ref[0, slot]
        tile = jnp.maximum(code - 1, 0)
        left, right = tile // NP, tile % NP
        scale = jnp.where(code > 0, scale_ref[0, 0], 0.0)
        damping = jnp.where(jnp.logical_and(left == right, code > 0), DAMPING, 0.0)
        for block, first in enumerate(starts):
            rows = min(ROW_BLOCK, P_SIZE - first)
            step = slot * len(starts) + block
            buffer = step % TILE_BUFFERS
            if step >= TILE_BUFFERS:
                write(step - TILE_BUFFERS).wait()
            gram = lax.dot_general(
                panels[left, :, first:first + ROW_BLOCK], panels[right],
                (((0,), (0,)), ((), ())), preferred_element_type=jnp.float32)
            factor = gram[:rows, :P_SIZE] * scale
            tiles[buffer, :rows, :] = factor
            last = min(first + ROW_BLOCK, P_SIZE)
            row = lax.broadcasted_iota(jnp.int32, (rows, last - first), 0)
            col = lax.broadcasted_iota(jnp.int32, (rows, last - first), 1)
            tiles[buffer, :rows, first:last] = (
                factor[:, first:last] + jnp.where(row == col, damping, 0.0))
            write(step).start()
    steps = slot_count * len(starts)
    for step in range(max(0, steps - TILE_BUFFERS), steps):
        write(step).wait()


def make_tiles(codes, panels, scale, slot_count):
    vmem = pl.BlockSpec(memory_space=pltpu.VMEM)
    return pl.pallas_call(
        functools.partial(tile_kernel, slot_count),
        out_shape=jax.ShapeDtypeStruct((slot_count, P_SIZE, P_SIZE), jnp.float32),
        in_specs=[pl.BlockSpec(memory_space=pltpu.SMEM), vmem, vmem],
        out_specs=pl.BlockSpec(memory_space=pl.ANY),
        scratch_shapes=[
            pltpu.VMEM((TILE_BUFFERS, ROW_BLOCK, P_SIZE), jnp.float32),
            pltpu.SemaphoreType.DMA((TILE_BUFFERS,)),
        ],
        compiler_params=pltpu.CompilerParams(vmem_limit_bytes=20 * 2**20),
        name="factor_tiles",
    )(codes, panels, scale)


def shards(grads, tile_slot):
    n = lax.axis_size("wide")
    slot_count = (TILES + n - 1) // n
    panels, codes, scale = gather(grads, tile_slot, n, slot_count)
    return make_tiles(codes, panels, scale, slot_count)


def solution(mesh):
    in_specs = (P(("parts", "wide"), None), P("parts"))
    out_specs = P(("parts", "wide"), None, None)
    return jax.shard_map(shards, mesh=mesh, in_specs=in_specs, out_specs=out_specs, check_vma=False)
```
